256 devices in a mesh: section: 16 (over z_lo, y, core), expert: 16 (over z_hi, x).
Axes of the slice: x: 4, y: 4, z: 8 (z_hi: 4, z_lo: 2; z = z_hi * 2 + z_lo), core: 2. Of those that a mesh axis runs over, the one named last changes fastest.
Arguments:
- tokens: bfloat16 [32768, 4096], P(('section', 'expert')), may hold values from -6 to 6
- norm_gain: float32 [16, 4096], P('section'), may hold values from 0.1 to 1.9
- w_gate: bfloat16 [16, 4096, 6144], P('section', None, 'expert'), may hold values from -0.09375 to 0.09375
- w_up: bfloat16 [16, 4096, 6144], P('section', None, 'expert'), may hold values from -0.09375 to 0.09375
- w_down: bfloat16 [16, 6144, 4096], P('section', 'expert'), may hold values from -0.21875 to 0.21875
- route_ids: int32 [2, 32768, 2], P(None, ('section', 'expert')), may hold values from 0 to 7, all different within a row; in each aligned block of 128 rows (0 to 127, 128 to 255, ..., all dimensions but the last counted through in order) at most 40 rows name the same one
- route_weights: bfloat16 [2, 32768, 2], P(None, ('section', 'expert')), may hold values from 0.25 to 1
Outputs:
- mixture: bfloat16 [32768, 4096], P(('section', 'expert'))
The draws below stay inside these ranges and needn't reach their ends.
Inputs may be any that keep to these rules, and one draw needn't show every extreme that they name: `route_ids`: in each aligned block of 128 rows of a loop step (the rows of one device), a row names 2 different experts, no expert is named by more than 40 rows, a bound that some block reaches.
All inputs are finite; a program needn't handle non-finite values.
Results may differ from the reference program's by a relative error of at most 0.0072.
Values may be sent and summed in bfloat16 or wider, within the bound.
No kernel may reach another device: no remote copies, remote signals or barrier semaphores. Data moves between devices by JAX's collectives and lax.ppermute only.
A program may use at most 64 MiB of HBM per device.

```python
import math
import jax
import jax.numpy as jnp
import numpy as np
from jax import lax

D = 4096
FF = 768
HALF = 384
TOPK = 2
ROWS = 128
STEPS = 2
EXPERTS = 8
MOST = 40
TOKENS = 32768
N_SECTION = 16
N_EXPERT = 16


def steps_of(rng, extent, split, least, top_value):
    def one(axis_at, shards_of):
        steps = jax.random.uniform(jax.random.fold_in(jax.random.fold_in(rng, 6), axis_at), (shards_of,), jnp.float32, least / len(split), top_value / len(split))
        return jnp.repeat(jnp.exp(steps), extent[axis_at] // shards_of).reshape((-1,) + (1,) * (len(extent) - axis_at - 1))

    level = one(*split[0])
    for cut in split[1:]:
        level = level * one(*cut)
    return level


def assign_block(own_key, own, number, rows, number_of, top, limit, lean):
    ranking = jax.random.permutation(own_key, number_of)
    crowded, ordinary = load_shares(number_of, rows * top, limit, lean, True), load_shares(number_of, rows * top, limit, lean, False)
    places = jnp.arange(number_of)

    def named(sizes, offset_by):
        used = int((sizes > 0).sum())
        fixed = max(1, used // 4)
        moved = fixed + (places - fixed + offset_by * (used - fixed)) % max(1, number_of - fixed)
        return jnp.zeros((number_of,), jnp.int32).at[ranking[jnp.where(places < fixed, places, moved)]].set(jnp.asarray(sizes, jnp.int32))

    sizes = jnp.where(number % 4 == 0, named(crowded, number // 4), named(ordinary, number - number // 4 - 1))
    mixed = jax.random.permutation(jax.random.fold_in(own, 3), number_of)
    source_of, taker = mixed[0:number_of // 2 * 2:2], mixed[1:number_of // 2 * 2:2]
    room = jnp.minimum(sizes[source_of] - 1, limit - sizes[taker]) // 2
    room = jnp.where((source_of == ranking[0]) | (taker == ranking[0]) | (sizes[taker] == 0), 0, jnp.maximum(room, 0))
    moved = jax.random.randint(jax.random.fold_in(own, 4), (number_of // 2,), 0, 1 << 20) % (room + 1)
    sizes = sizes.at[source_of].add(-moved).at[taker].add(moved)
    labels = jnp.searchsorted(jnp.cumsum(sizes), jnp.arange(rows * top), side="right").astype(jnp.int32)
    grid = labels.reshape(top, rows).T
    grid = grid[jax.random.permutation(jax.random.fold_in(own, 1), rows)]
    offset_by = jax.random.randint(jax.random.fold_in(own, 2), (rows, 1), 0, top)
    return jnp.take_along_axis(grid, (jnp.arange(top)[None, :] + offset_by) % top, axis=1)


def load_shares(number_of, total, bound, lean, full):
    weights = [(1 << 20) // math.isqrt(standing ** lean) + 1 for standing in range(1, number_of + 1)]
    largest = bound if full else min(bound, max(-(-total // number_of), total * weights[0] // sum(weights)))
    least = 1 if total - largest >= number_of - 1 else 0
    given, spare = [largest] + [least] * (number_of - 1), total - largest - least * (number_of - 1)
    while spare > 0:
        candidates = [i for i in range(1, number_of) if given[i] < largest] or [i for i in range(1, number_of) if given[i] < bound]
        whole, budget = sum([weights[i] for i in candidates]), spare
        for i in candidates:
            addition = min(bound - given[i], max(1, budget * weights[i] // whole), spare)
            given[i] = given[i] + addition
            spare = spare - addition
    return np.array(given)


def normal_values(key, dims, spread, limit, cuts=(), kind=jnp.bfloat16):
    loudness = steps_of(key, dims, cuts, -0.22, 0.18) if cuts else 1.0
    values = jax.random.normal(key, dims, jnp.float32) * spread * loudness
    return jnp.minimum(jnp.maximum(values, -limit), limit).astype(kind)


def setup_inputs(seed: int = 0) -> dict:
    key_of = jax.random.split(jax.random.key(seed), 8)
    tokens = normal_values(key_of[0], (TOKENS, D), 1.0, 6.0, ((0, 256),))
    norm_gain = jnp.clip(1.0 + 0.18 * jax.random.normal(key_of[1], (N_SECTION, D), jnp.float32), 0.1, 1.9)
    w_gate = normal_values(key_of[2], (N_SECTION, D, EXPERTS * FF), D ** -0.5, 0.09375, ((0, 16), (2, 16)))
    w_up = normal_values(key_of[3], (N_SECTION, D, EXPERTS * FF), D ** -0.5, 0.09375, ((0, 16), (2, 16)))
    w_down = normal_values(key_of[4], (N_SECTION, EXPERTS * FF, D), FF ** -0.5, 0.21875, ((0, 16), (1, 16)))
    route_ids_keys = jax.random.split(jax.random.fold_in(key_of[5], 1), STEPS * TOKENS // ROWS)
    route_ids_turns = jax.random.permutation(jax.random.fold_in(key_of[5], 3), STEPS * TOKENS // ROWS)
    route_ids = jax.vmap(lambda own, number: assign_block(jax.random.fold_in(key_of[5], 2), own, number, ROWS, EXPERTS, TOPK, MOST, 2))(route_ids_keys, route_ids_turns).reshape((STEPS, TOKENS, TOPK))
    route_weights = jnp.clip(0.25 + 0.75 * jax.random.uniform(key_of[6], (STEPS, TOKENS, TOPK), jnp.float32) ** steps_of(key_of[6], (STEPS, TOKENS, TOPK), ((1, 256),), -0.2, 0.2), 0.25, 1.0).astype(jnp.bfloat16)
    return {"tokens": tokens, "norm_gain": norm_gain, "w_gate": w_gate, "w_up": w_up, "w_down": w_down, "route_ids": route_ids, "route_weights": route_weights}


def rms_norm(values, gain):
    wide = values.astype(jnp.float32)
    meansq = lax.optimization_barrier(jnp.mean(wide * wide, axis=-1, keepdims=True))
    return (wide * lax.rsqrt(meansq + 1e-06) * gain.astype(jnp.float32)).astype(jnp.bfloat16)

def slot_tables(ids, weights, experts, capacity):
    flat_ids = ids.reshape(-1)
    expert_range = jnp.arange(experts, dtype=jnp.int32)
    hot = (flat_ids[:, None] == expert_range[None, :]).astype(jnp.int32)
    ranks = jnp.cumsum(hot, axis=0) - 1
    slots = lax.optimization_barrier(jnp.sum(hot * ranks, axis=1)).reshape(ids.shape)
    hit_expert = (ids[:, :, None] == expert_range[None, None, :]).astype(jnp.float32)
    slot_range = jnp.arange(capacity, dtype=jnp.int32)
    hit_slot = (slots[:, :, None] == slot_range[None, None, :]).astype(jnp.float32)
    select = jnp.einsum('rke,rkc->ecr', hit_expert, hit_slot)
    combine = jnp.einsum('rke,rkc,rk->rec', hit_expert, hit_slot, weights.astype(jnp.float32))
    return (select, combine)

def section_layer(block_rows, gain, gates, ups, downs, ids, weights):
    normed = rms_norm(block_rows, gain).reshape(N_EXPERT, ROWS, D)
    select, combine = jax.vmap(lambda one_ids, one_weights: slot_tables(one_ids, one_weights, EXPERTS, MOST))(ids, weights)
    inputs = jnp.einsum('becr,brd->ebcd', select, normed.astype(jnp.float32)).astype(jnp.bfloat16)

    def one_expert(packed):
        rows_in, gate_w, up_w, down_w = packed
        flat_rows = rows_in.reshape(-1, D)
        gate_proj = jnp.dot(flat_rows, gate_w, preferred_element_type=jnp.float32)
        up_proj = jnp.dot(flat_rows, up_w, preferred_element_type=jnp.float32)
        hidden = (jax.nn.silu(gate_proj) * up_proj).astype(jnp.bfloat16)
        low_part = jnp.dot(hidden[:, :HALF], down_w[:HALF], preferred_element_type=jnp.float32).astype(jnp.bfloat16)
        high_part = jnp.dot(hidden[:, HALF:], down_w[HALF:], preferred_element_type=jnp.float32).astype(jnp.bfloat16)
        summed = (low_part.astype(jnp.float32) + high_part.astype(jnp.float32)).astype(jnp.bfloat16)
        return summed.reshape(N_EXPERT, MOST, D)
    outputs = lax.map(one_expert, (inputs, gates, ups, downs))
    mixed = jnp.einsum('brec,ebcd->brd', combine, outputs.astype(jnp.float32))
    return (block_rows.astype(jnp.float32) + mixed.reshape(N_EXPERT * ROWS, D)).astype(jnp.bfloat16)

def reference(tokens, norm_gain, w_gate, w_up, w_down, route_ids, route_weights):
    state = tokens.reshape(N_SECTION, N_EXPERT * ROWS, D)
    gates = w_gate.reshape(N_SECTION, D, EXPERTS, FF).transpose(0, 2, 1, 3)
    ups = w_up.reshape(N_SECTION, D, EXPERTS, FF).transpose(0, 2, 1, 3)
    downs = w_down.reshape(N_SECTION, EXPERTS, FF, D)
    for loop_step in range(STEPS):
        ids_now = route_ids[loop_step].reshape(N_SECTION, N_EXPERT, ROWS, TOPK)
        weights_now = route_weights[loop_step].reshape(N_SECTION, N_EXPERT, ROWS, TOPK)
        state = lax.map(lambda packed: section_layer(*packed), (state, norm_gain, gates, ups, downs, ids_now, weights_now))
        state = jnp.roll(state, 1, axis=0)
    return state.reshape(TOKENS, D)
```

```python
import jax
import jax.numpy as jnp
from jax import lax
from jax.sharding import PartitionSpec as P

D = 4096
SLOTS = 40
NX = 4
NZ = 4
CHUNKS = (((0,), 0, 40), ((2,), 0, 40), ((1, 3), 0, 24), ((1, 3), 24, 16))


def expert_at(z, x):
    return (z % NZ) * NX + (x % NX)


def along_x(block, flip):
    route = [(expert_at(z, x), expert_at(z, x ^ flip)) for z in range(NZ) for x in range(NX)]
    return lax.ppermute(block, "expert", route)


def along_z(block, distance):
    route = [(expert_at(z, x), expert_at(z + distance, x)) for z in range(NZ) for x in range(NX)]
    return lax.ppermute(block, "expert", route)


def to_next(block, distance):
    sections = lax.axis_size("section")
    if distance == 0:
        return lax.ppermute(block, "section", [(s, (s + 1) % sections) for s in range(sections)])
    route = [
        (s * NZ * NX + expert_at(z, x), (s + 1) % sections * NZ * NX + expert_at(z + distance, x))
        for s in range(sections)
        for z in range(NZ)
        for x in range(NX)
    ]
    return lax.ppermute(block, ("section", "expert"), route)


def rms_norm(values, gain):
    wide = values.astype(jnp.float32)
    meansq = jnp.mean(wide * wide, axis=-1, keepdims=True)
    return (wide * lax.rsqrt(meansq + 1e-06) * gain).astype(jnp.bfloat16)


def blocks_of():
    return [(k, first, count) for ks, first, count in CHUNKS for k in ks]


def tables(ids, weights):
    rows = ids.shape[0]
    z = lax.axis_index("expert") // NX
    pair = lax.axis_index("expert") % NX // 2
    experts = jnp.arange(2 * NZ, dtype=jnp.int32)
    hit_k = ids[:, :, None] == experts
    hit = jnp.any(hit_k, axis=1)
    share = jnp.sum(jnp.where(hit_k, weights.astype(jnp.float32)[:, :, None], 0.0), axis=1)
    before = jnp.tril(jnp.ones((rows, rows), jnp.bfloat16), -1)
    ranks = jnp.dot(before, hit.astype(jnp.bfloat16), preferred_element_type=jnp.float32)
    code = jnp.where(hit, ranks, -1.0)
    places, slots = [], []
    for k, first, count in blocks_of():
        for other in range(2):
            places += [(k, other)] * count
            slots += list(range(first, first + count))
    ks = jnp.array([p[0] for p in places], jnp.int32)
    others = jnp.array([p[1] for p in places], jnp.int32)
    named = 2 * ((z + ks) % NZ) + (pair ^ others)
    hot = (named[:, None] == experts).astype(jnp.bfloat16)
    code_at = lax.dot_general(hot, code.astype(jnp.bfloat16), (((1,), (1,)), ((), ())), preferred_element_type=jnp.float32)
    share_at = lax.dot_general(hot, share.astype(jnp.bfloat16), (((1,), (1,)), ((), ())), preferred_element_type=jnp.float32)
    match = code_at == jnp.array(slots, jnp.float32)[:, None]
    select = match.astype(jnp.bfloat16)
    combine = jnp.where(match, share_at, 0.0).astype(jnp.bfloat16)
    return select, combine


def fence(*values):
    return lax.optimization_barrier(values)


def hidden_rows(rows, weights):
    gate = jnp.dot(rows, weights[0], preferred_element_type=jnp.float32)
    up = jnp.dot(rows, weights[1], preferred_element_type=jnp.float32)
    return (jax.nn.silu(gate) * up).astype(jnp.bfloat16)


def down_rows(hidden, got, both_down):
    both = jnp.concatenate([hidden, got], axis=1)
    out = jnp.dot(both, both_down, preferred_element_type=jnp.float32).astype(jnp.bfloat16)
    return jnp.split(out, 2, axis=0)


def gather_pair(blocks):
    count = blocks[0].shape[0] // 2
    own = [b[:count] for b in blocks]
    other = [b[count:] for b in blocks]
    if len(blocks) == 1:
        return own[0], other[0]
    return jnp.concatenate(own, axis=0), jnp.concatenate(other, axis=0)


def across(blocks):
    own, other = gather_pair(blocks)
    return jnp.concatenate([own, along_x(other, 3)], axis=0)


def section_layer(state, gain, weights, both_down, ids, shares, first):
    select, combine = tables(ids, shares)
    normed = rms_norm(state, gain)
    picked = jnp.dot(select, normed, preferred_element_type=jnp.float32).astype(jnp.bfloat16)
    parts = []
    at = 0
    for _, _, count in blocks_of():
        parts.append(picked[at : at + 2 * count])
        at += 2 * count
    p_own, p_two, p_a1, p_a3, p_b1, p_b3 = parts

    two = along_z(p_two, 2)
    rows_own = across([p_own])
    near_own = rows_own if first else along_x(rows_own, 1)
    two, rows_own, near_own, combine, state, p_a1, p_a3 = fence(two, rows_own, near_own, combine, state, p_a1, p_a3)
    a1 = along_z(p_a1, 1)
    a3 = along_z(p_a3, -1)
    rows_two = across([two])
    combine = to_next(combine, 0)
    a1, a3, rows_two, combine, p_b1, p_b3 = fence(a1, a3, rows_two, combine, p_b1, p_b3)
    b1 = along_z(p_b1, 1)
    b3 = along_z(p_b3, -1)
    near_two = along_x(rows_two, 1)
    rows_a = across([a1, a3])
    b1, b3, near_two, rows_two, rows_a, near_own, state, both_down = fence(
        b1, b3, near_two, rows_two, rows_a, near_own, state, both_down
    )
    near_a = along_x(rows_a, 1)
    next_state = to_next(state, 0)
    got_two = along_x(hidden_rows(near_two, weights), 1)
    rows_b = across([b1, b3])
    done_two, far_two = down_rows(hidden_rows(rows_two, weights), got_two, both_down)
    done_two, far_two, rows_b = fence(done_two, far_two, rows_b)
    r_two = to_next(done_two, -2)
    far_two = along_x(far_two, 3)
    near_a, rows_a, rows_b, rows_own, near_own, r_two, far_two = fence(
        near_a, rows_a, rows_b, rows_own, near_own, r_two, far_two
    )
    f_two = to_next(far_two, -2)
    near_b = along_x(rows_b, 1)
    got_a = along_x(hidden_rows(near_a, weights), 1)
    near_own = along_x(rows_own, 1) if first else near_own
    hid_a = hidden_rows(rows_a, weights)
    f_two, near_b, rows_b, got_a, hid_a, near_own, rows_own, next_state = fence(
        f_two, near_b, rows_b, got_a, hid_a, near_own, rows_own, next_state
    )
    done_a, far_a = down_rows(hid_a, got_a, both_down)
    got_b = along_x(hidden_rows(near_b, weights), 1)
    got_own = along_x(hidden_rows(near_own, weights), 1)
    half = done_a.shape[0] // 2
    r_a1 = to_next(done_a[:half], -1)
    r_a3 = to_next(done_a[half:], 1)
    far_a = along_x(far_a, 3)
    hid_b = hidden_rows(rows_b, weights)
    hid_own = hidden_rows(rows_own, weights)
    r_a1, r_a3, far_a, got_b, got_own, hid_b, hid_own = fence(r_a1, r_a3, far_a, got_b, got_own, hid_b, hid_own)
    f_a1 = to_next(far_a[:half], -1)
    f_a3 = to_next(far_a[half:], 1)
    done_b, far_b = down_rows(hid_b, got_b, both_down)
    far_b = along_x(far_b, 3)
    done_own, far_own = down_rows(hid_own, got_own, both_down)
    r_own = to_next(done_own, 0)
    far_own = along_x(far_own, 3)
    f_a1, f_a3, done_b, far_b, r_own, far_own = fence(f_a1, f_a3, done_b, far_b, r_own, far_own)
    half = done_b.shape[0] // 2
    r_b1 = to_next(done_b[:half], -1)
    r_b3 = to_next(done_b[half:], 1)
    f_b1 = to_next(far_b[:half], -1)
    f_b3 = to_next(far_b[half:], 1)
    f_own = to_next(far_own, 0)
    merged = jnp.concatenate(
        [r_own, f_own, r_two, f_two, r_a1, f_a1, r_a3, f_a3, r_b1, f_b1, r_b3, f_b3], axis=0
    )
    mixed = lax.dot_general(combine, merged, (((0,), (0,)), ((), ())), preferred_element_type=jnp.float32)
    return (next_state.astype(jnp.float32) + mixed).astype(jnp.bfloat16)


def per_device(tokens, norm_gain, w_gate, w_up, w_down, route_ids, route_weights):
    state = tokens
    weights = (w_gate[0], w_up[0])
    both_down = jnp.concatenate([w_down[0], along_x(w_down[0], 1)], axis=0)
    for t in range(route_ids.shape[0]):
        state = section_layer(state, norm_gain[0], weights, both_down, route_ids[t], route_weights[t], t == 0)
    return state


def solution(mesh):
    in_specs = (
        P(("section", "expert"), None),
        P("section", None),
        P("section", None, "expert"),
        P("section", None, "expert"),
        P("section", "expert", None),
        P(None, ("section", "expert"), None),
        P(None, ("section", "expert"), None),
    )
    out_specs = P(("section", "expert"), None)
    return jax.shard_map(
        per_device, mesh=mesh, in_specs=in_specs, out_specs=out_specs, check_vma=False
    )
```

```python
import jax
import jax.numpy as jnp
from jax import lax
from jax.sharding import PartitionSpec as P

D = 4096
SLOTS = 40
NX = 4
NZ = 4
DISTANCES = (0, 2, 1, 3)


def expert_at(z, x):
    return (z % NZ) * NX + (x % NX)


def along_x(block, flip):
    route = [(expert_at(z, x), expert_at(z, x ^ flip)) for z in range(NZ) for x in range(NX)]
    return lax.ppermute(block, "expert", route)


def along_z(block, distance):
    route = [(expert_at(z, x), expert_at(z + distance, x)) for z in range(NZ) for x in range(NX)]
    return lax.ppermute(block, "expert", route)


def to_next(block, distance):
    sections = lax.axis_size("section")
    if distance == 0:
        return lax.ppermute(block, "section", [(s, (s + 1) % sections) for s in range(sections)])
    route = [
        (s * NZ * NX + expert_at(z, x), (s + 1) % sections * NZ * NX + expert_at(z + distance, x))
        for s in range(sections)
        for z in range(NZ)
        for x in range(NX)
    ]
    return lax.ppermute(block, ("section", "expert"), route)


def rms_norm(values, gain):
    wide = values.astype(jnp.float32)
    meansq = jnp.mean(wide * wide, axis=-1, keepdims=True)
    return (wide * lax.rsqrt(meansq + 1e-06) * gain).astype(jnp.bfloat16)


def tables(ids, weights):
    rows = ids.shape[0]
    z = lax.axis_index("expert") // NX
    pair = lax.axis_index("expert") % NX // 2
    experts = jnp.arange(2 * NZ, dtype=jnp.int32)
    hit_k = ids[:, :, None] == experts
    hit = jnp.any(hit_k, axis=1)
    share = jnp.sum(jnp.where(hit_k, weights.astype(jnp.float32)[:, :, None], 0.0), axis=1)
    before = jnp.tril(jnp.ones((rows, rows), jnp.bfloat16), -1)
    ranks = jnp.dot(before, hit.astype(jnp.bfloat16), preferred_element_type=jnp.float32)
    code = jnp.where(hit, ranks, -1.0)
    ks = jnp.repeat(jnp.array(DISTANCES, jnp.int32), 2 * SLOTS)
    others = jnp.tile(jnp.repeat(jnp.arange(2, dtype=jnp.int32), SLOTS), NZ)
    slots = jnp.tile(jnp.arange(SLOTS, dtype=jnp.float32), 2 * NZ)
    named = 2 * ((z + ks) % NZ) + (pair ^ others)
    hot = (named[:, None] == experts).astype(jnp.bfloat16)
    code_at = lax.dot_general(hot, code.astype(jnp.bfloat16), (((1,), (1,)), ((), ())), preferred_element_type=jnp.float32)
    share_at = lax.dot_general(hot, share.astype(jnp.bfloat16), (((1,), (1,)), ((), ())), preferred_element_type=jnp.float32)
    match = code_at == slots[:, None]
    select = match.astype(jnp.bfloat16)
    combine = jnp.where(match, share_at, 0.0).astype(jnp.bfloat16)
    return select, combine


def fence(*values):
    return lax.optimization_barrier(values)


def hidden_rows(rows, weights):
    gate = jnp.dot(rows, weights[0], preferred_element_type=jnp.float32)
    up = jnp.dot(rows, weights[1], preferred_element_type=jnp.float32)
    return (jax.nn.silu(gate) * up).astype(jnp.bfloat16)


def down_rows(hidden, got, both_down):
    both = jnp.concatenate([hidden, got], axis=1)
    out = jnp.dot(both, both_down, preferred_element_type=jnp.float32).astype(jnp.bfloat16)
    return jnp.split(out, 2, axis=0)


def both(*blocks):
    return jnp.concatenate(blocks, axis=0)


def section_layer(state, gain, weights, downs, ids, shares, first):
    select, combine = tables(ids, shares)
    normed = rms_norm(state, gain)
    picked = jnp.dot(select, normed, preferred_element_type=jnp.float32).astype(jnp.bfloat16)
    p_own, p_two, p_one, p_three = jnp.split(picked, 4, axis=0)
    own, other_own = jnp.split(p_own, 2, axis=0)

    two = along_z(p_two, 2)
    combine = to_next(combine, 0)
    cross = along_x(other_own, 3)
    if first:
        two, own, cross, combine, state, p_one, p_three = fence(two, own, cross, combine, state, p_one, p_three)
        rows_own = both(own, cross)
        hid_own = hidden_rows(rows_own, weights)
    else:
        near = along_x(own, 1)
        far = along_x(other_own, 2)
        own, cross, near, far = fence(own, cross, near, far)
        got_own = along_x(hidden_rows(both(near, far), weights), 1)
        hid_own = hidden_rows(both(own, cross), weights)
        two, got_own, hid_own, combine, state, p_one, p_three = fence(
            two, got_own, hid_own, combine, state, p_one, p_three
        )
    one = along_z(p_one, 1)
    three = along_z(p_three, -1)
    own, other = jnp.split(two, 2, axis=0)
    cross = along_x(other, 3)
    if first:
        own, cross, state, rows_own, hid_own = fence(own, cross, state, rows_own, hid_own)
        rows_two = both(own, cross)
        near_two = along_x(rows_two, 1)
        one, three, state, rows_two = fence(one, three, state, rows_two)
        next_state = to_next(state, 0)
        own = both(one[:SLOTS], three[:SLOTS])
        cross = along_x(both(one[SLOTS:], three[SLOTS:]), 3)
        hid_two = hidden_rows(rows_two, weights)
        got_two = along_x(hidden_rows(near_two, weights), 1)
        own, cross, got_two, hid_two, downs, rows_own = fence(own, cross, got_two, hid_two, downs, rows_own)
        rows_far = both(own, cross)
        near_far = along_x(rows_far, 1)
        both_down = both(*downs)
        done_two, far_two = down_rows(hid_two, got_two, both_down)
        far_two = along_x(far_two, 3)
        near_own = along_x(rows_own, 1)
        done_two, far_two, next_state = fence(done_two, far_two, next_state)
        r_two = to_next(both(done_two, far_two), -2)
        got_own = along_x(hidden_rows(near_own, weights), 1)
        hid_far = hidden_rows(rows_far, weights)
        done_own, far_own = down_rows(hid_own, got_own, both_down)
        r_two, near_far, done_own, far_own, hid_far = fence(r_two, near_far, done_own, far_own, hid_far)
        far_own = along_x(far_own, 3)
        own = cross = None
    else:
        near = along_x(own, 1)
        far = along_x(other, 2)
        both_down = downs
        done_own, far_own = down_rows(hid_own, got_own, both_down)
        own, cross, near, far, done_own, far_own = fence(own, cross, near, far, done_own, far_own)
        far_own = along_x(far_own, 3)
        got_two = along_x(hidden_rows(both(near, far), weights), 1)
        hid_two = hidden_rows(both(own, cross), weights)
        done_two, far_two = down_rows(hid_two, got_two, both_down)
        far_two = along_x(far_two, 3)
        one, three, state, done_two, far_two, done_own, far_own = fence(
            one, three, state, done_two, far_two, done_own, far_own
        )
        r_two = to_next(both(done_two, far_two), -2)
        own = both(one[:SLOTS], three[:SLOTS])
        other = both(one[SLOTS:], three[SLOTS:])
        cross = along_x(other, 3)
        near = along_x(own, 1)
        far = along_x(other, 2)
        next_state = to_next(state, 0)
        r_two, own, cross, near, far = fence(r_two, own, cross, near, far)
        near_far = both(near, far)
    got_far = along_x(hidden_rows(near_far, weights), 1)
    if not first:
        hid_far = hidden_rows(both(own, cross), weights)
    done, far = down_rows(hid_far, got_far, both_down)
    r_one = to_next(done[:SLOTS], -1)
    r_three = to_next(done[SLOTS:], 1)
    far = along_x(far, 3)
    r_own = to_next(both(done_own, far_own), 0)
    r_one, r_three, far, next_state, r_own = fence(r_one, r_three, far, next_state, r_own)
    f_one = to_next(far[:SLOTS], -1)
    f_three = to_next(far[SLOTS:], 1)
    merged = both(r_own, r_two, r_one, f_one, r_three, f_three)
    mixed = lax.dot_general(combine, merged, (((0,), (0,)), ((), ())), preferred_element_type=jnp.float32)
    return (next_state.astype(jnp.float32) + mixed).astype(jnp.bfloat16), both_down


def per_device(tokens, norm_gain, w_gate, w_up, w_down, route_ids, route_weights):
    state = tokens
    weights = (w_gate[0], w_up[0])
    downs = (w_down[0], along_x(w_down[0], 1))
    for t in range(route_ids.shape[0]):
        state, downs = section_layer(state, norm_gain[0], weights, downs, route_ids[t], route_weights[t], t == 0)
    return state


def solution(mesh):
    in_specs = (
        P(("section", "expert"), None),
        P("section", None),
        P("section", None, "expert"),
        P("section", None, "expert"),
        P("section", "expert", None),
        P(None, ("section", "expert"), None),
        P(None, ("section", "expert"), None),
    )
    out_specs = P(("section", "expert"), None)
    return jax.shard_map(
        per_device, mesh=mesh, in_specs=in_specs, out_specs=out_specs, check_vma=False
    )
```

```python
import jax
import jax.numpy as jnp
from jax import lax
from jax.sharding import PartitionSpec as P

D = 4096
SLOTS = 40
NX = 4
NZ = 4
DISTANCES = (0, 2, 1, 3)


def expert_at(z, x):
    return (z % NZ) * NX + (x % NX)


def along_x(block, flip):
    route = [(expert_at(z, x), expert_at(z, x ^ flip)) for z in range(NZ) for x in range(NX)]
    return lax.ppermute(block, "expert", route)


def along_z(block, distance):
    route = [(expert_at(z, x), expert_at(z + distance, x)) for z in range(NZ) for x in range(NX)]
    return lax.ppermute(block, "expert", route)


def to_next(block, distance):
    sections = lax.axis_size("section")
    if distance == 0:
        return lax.ppermute(block, "section", [(s, (s + 1) % sections) for s in range(sections)])
    route = [
        (s * NZ * NX + expert_at(z, x), (s + 1) % sections * NZ * NX + expert_at(z + distance, x))
        for s in range(sections)
        for z in range(NZ)
        for x in range(NX)
    ]
    return lax.ppermute(block, ("section", "expert"), route)


def rms_norm(values, gain):
    wide = values.astype(jnp.float32)
    meansq = jnp.mean(wide * wide, axis=-1, keepdims=True)
    return (wide * lax.rsqrt(meansq + 1e-06) * gain).astype(jnp.bfloat16)


def tables(ids, weights):
    rows = ids.shape[0]
    z = lax.axis_index("expert") // NX
    pair = lax.axis_index("expert") % NX // 2
    experts = jnp.arange(2 * NZ, dtype=jnp.int32)
    hit_k = ids[:, :, None] == experts
    hit = jnp.any(hit_k, axis=1)
    share = jnp.sum(jnp.where(hit_k, weights.astype(jnp.float32)[:, :, None], 0.0), axis=1)
    before = jnp.tril(jnp.ones((rows, rows), jnp.bfloat16), -1)
    ranks = jnp.dot(before, hit.astype(jnp.bfloat16), preferred_element_type=jnp.float32)
    code = jnp.where(hit, ranks, -1.0)
    ks = jnp.repeat(jnp.array(DISTANCES, jnp.int32), 2 * SLOTS)
    others = jnp.tile(jnp.repeat(jnp.arange(2, dtype=jnp.int32), SLOTS), NZ)
    slots = jnp.tile(jnp.arange(SLOTS, dtype=jnp.float32), 2 * NZ)
    named = 2 * ((z + ks) % NZ) + (pair ^ others)
    hot = (named[:, None] == experts).astype(jnp.bfloat16)
    code_at = lax.dot_general(hot, code.astype(jnp.bfloat16), (((1,), (1,)), ((), ())), preferred_element_type=jnp.float32)
    share_at = lax.dot_general(hot, share.astype(jnp.bfloat16), (((1,), (1,)), ((), ())), preferred_element_type=jnp.float32)
    match = code_at == slots[:, None]
    select = match.astype(jnp.bfloat16)
    combine = jnp.where(match, share_at, 0.0).astype(jnp.bfloat16)
    return select, combine


def fence(*values):
    return lax.optimization_barrier(values)


def hidden_rows(rows, weights):
    gate = jnp.dot(rows, weights[0], preferred_element_type=jnp.float32)
    up = jnp.dot(rows, weights[1], preferred_element_type=jnp.float32)
    return (jax.nn.silu(gate) * up).astype(jnp.bfloat16)


def down_rows(hidden, got, both_down):
    both = jnp.concatenate([hidden, got], axis=1)
    out = jnp.dot(both, both_down, preferred_element_type=jnp.float32).astype(jnp.bfloat16)
    return jnp.split(out, 2, axis=0)


def both(*blocks):
    return jnp.concatenate(blocks, axis=0)


def section_layer(state, gain, weights, downs, ids, shares, first):
    select, combine = tables(ids, shares)
    normed = rms_norm(state, gain)
    picked = jnp.dot(select, normed, preferred_element_type=jnp.float32).astype(jnp.bfloat16)
    p_own, p_two, p_one, p_three = jnp.split(picked, 4, axis=0)
    own, other_own = jnp.split(p_own, 2, axis=0)

    two = along_z(p_two, 2)
    if not first:
        combine = to_next(combine, 0)
    cross = along_x(other_own, 3)
    if first:
        two, own, cross, combine, state, p_one, p_three = fence(two, own, cross, combine, state, p_one, p_three)
        rows_own = both(own, cross)
        hid_own = hidden_rows(rows_own, weights)
    else:
        near = along_x(own, 1)
        far = along_x(other_own, 2)
        own, cross, near, far = fence(own, cross, near, far)
        got_own = along_x(hidden_rows(both(near, far), weights), 1)
        hid_own = hidden_rows(both(own, cross), weights)
        two, got_own, hid_own, combine, state, p_one, p_three = fence(
            two, got_own, hid_own, combine, state, p_one, p_three
        )
    one = along_z(p_one, 1)
    three = along_z(p_three, -1)
    own, other = jnp.split(two, 2, axis=0)
    cross = along_x(other, 3)
    if first:
        combine = to_next(combine, 0)
        own, cross, state, rows_own, hid_own = fence(own, cross, state, rows_own, hid_own)
        rows_two = both(own, cross)
        near_two = along_x(rows_two, 1)
        one, three, state, rows_two, combine = fence(one, three, state, rows_two, combine)
        next_state = to_next(state, 0)
        own = both(one[:SLOTS], three[:SLOTS])
        cross = along_x(both(one[SLOTS:], three[SLOTS:]), 3)
        hid_two = hidden_rows(rows_two, weights)
        got_two = along_x(hidden_rows(near_two, weights), 1)
        both_down = both(*downs)
        own, cross, got_two, hid_two, both_down, rows_own = fence(own, cross, got_two, hid_two, both_down, rows_own)
        rows_far = both(own, cross)
        near_far = along_x(rows_far, 1)
        done_two, far_two = down_rows(hid_two, got_two, both_down)
        far_two = along_x(far_two, 3)
        near_own = along_x(rows_own, 1)
        done_two, far_two, next_state = fence(done_two, far_two, next_state)
        r_two = to_next(both(done_two, far_two), -2)
        got_own = along_x(hidden_rows(near_own, weights), 1)
        hid_far = hidden_rows(rows_far, weights)
        done_own, far_own = down_rows(hid_own, got_own, both_down)
        r_two, near_far, done_own, far_own, hid_far = fence(r_two, near_far, done_own, far_own, hid_far)
    else:
        near = along_x(own, 1)
        far = along_x(other, 2)
        both_down = downs
        done_own, far_own = down_rows(hid_own, got_own, both_down)
        own, cross, near, far, done_own, far_own = fence(own, cross, near, far, done_own, far_own)
        far_own = along_x(far_own, 3)
        got_two = along_x(hidden_rows(both(near, far), weights), 1)
        hid_two = hidden_rows(both(own, cross), weights)
        done_two, far_two = down_rows(hid_two, got_two, both_down)
        far_two = along_x(far_two, 3)
        one, three, state, done_two, far_two, done_own, far_own = fence(
            one, three, state, done_two, far_two, done_own, far_own
        )
        r_two = to_next(both(done_two, far_two), -2)
        own = both(one[:SLOTS], three[:SLOTS])
        other = both(one[SLOTS:], three[SLOTS:])
        cross = along_x(other, 3)
        near = along_x(own, 1)
        far = along_x(other, 2)
        next_state = to_next(state, 0)
        r_two, own, cross, near, far = fence(r_two, own, cross, near, far)
        near_far = both(near, far)
    got_far = along_x(hidden_rows(near_far, weights), 1)
    if not first:
        hid_far = hidden_rows(both(own, cross), weights)
    done, far = down_rows(hid_far, got_far, both_down)
    r_one = to_next(done[:SLOTS], -1)
    r_three = to_next(done[SLOTS:], 1)
    far = along_x(far, 3)
    if first:
        far_own = along_x(far_own, 3)
        r_one, r_three, far, done_own, far_own = fence(r_one, r_three, far, done_own, far_own)
        r_own = to_next(both(done_own, far_own), 0)
    else:
        r_own = to_next(both(done_own, far_own), 0)
        r_one, r_three, far, next_state, r_own = fence(r_one, r_three, far, next_state, r_own)
    f_one = to_next(far[:SLOTS], -1)
    f_three = to_next(far[SLOTS:], 1)
    merged = both(r_own, r_two, r_one, f_one, r_three, f_three)
    mixed = lax.dot_general(combine, merged, (((0,), (0,)), ((), ())), preferred_element_type=jnp.float32)
    return (next_state.astype(jnp.float32) + mixed).astype(jnp.bfloat16), both_down


def per_device(tokens, norm_gain, w_gate, w_up, w_down, route_ids, route_weights):
    state = tokens
    weights = (w_gate[0], w_up[0])
    downs = (w_down[0], along_x(w_down[0], 1))
    for t in range(route_ids.shape[0]):
        state, downs = section_layer(state, norm_gain[0], weights, downs, route_ids[t], route_weights[t], t == 0)
    return state


def solution(mesh):
    in_specs = (
        P(("section", "expert"), None),
        P("section", None),
        P("section", None, "expert"),
        P("section", None, "expert"),
        P("section", "expert", None),
        P(None, ("section", "expert"), None),
        P(None, ("section", "expert"), None),
    )
    out_specs = P(("section", "expert"), None)
    return jax.shard_map(
        per_device, mesh=mesh, in_specs=in_specs, out_specs=out_specs, check_vma=False
    )
```
